256 devices in a mesh: rep: 32 (over x, z_lo, core), shard: 8 (over z_hi, y).
Axes of the slice: x: 4, y: 4, z: 8 (z_hi: 2, z_lo: 4; z = z_hi * 4 + z_lo), core: 2. Of those that a mesh axis runs over, the one named last changes fastest.
Arguments:
- hidden_in: bfloat16 [32, 2048, 5120], P('rep', 'shard'), may hold values from -6 to 6
- cotangent: bfloat16 [32, 2048, 1024], P('rep', 'shard'), may hold values from -0.119628906 to 0.119628906
- token_ids: int32 [32, 2048], P('rep', 'shard'), may hold values from 0 to 152063, as said below
- params: float32 [32, 5120, 1024], P('rep', 'shard'), may hold values from -3 to 3
- momentum: bfloat16 [32, 5120, 1024], P('rep', 'shard'), may hold values from -6 to 6
- step_index: int32 [], replicated, may hold values from 0 to 63
Outputs:
- new_params: float32 [32, 5120, 1024], P('rep', 'shard')
- new_momentum: bfloat16 [32, 5120, 1024], P('rep', 'shard')
The draws below stay inside these ranges and needn't reach their ends.
Inputs may be any that keep to these rules, and one draw needn't show every extreme that they name: `token_ids`: id 0 marks padding; other ids are in 1 to 152063.
All inputs are finite; a program needn't handle non-finite values.
Results may differ from the reference program's by a relative error of at most 0.015.
Values may be sent and summed in bfloat16 or wider, within the bound.
A program may use at most 128 MiB of HBM per device.

```python
import jax
import jax.numpy as jnp
from jax import lax

D = 5120
KV_WIDTH = 1024
VOCAB = 152064
TOK_DEV = 256
TOK_REP = 2048
N_REP = 32
N_SHARD = 8


def draw_token_ids(key, part):
    key = jax.random.fold_in(key, 7)
    first, second = jax.random.split(key)
    words = jax.random.randint(first, (N_REP, TOK_REP), 1, VOCAB)
    pads = jax.random.randint(second, (N_REP, TOK_REP), 0, 4)
    ids = jnp.where(pads == 0, 0, words)
    ids = ids.at[0, 0].set(0).at[0, 1].set(VOCAB - 1)
    return ids.astype(jnp.int32)


def level_of(own_key, shape, shards, low, high):
    def one(position, shards_of):
        draws = jax.random.uniform(jax.random.fold_in(jax.random.fold_in(own_key, 6), position), (shards_of,), jnp.float32, low / len(shards), high / len(shards))
        return jnp.repeat(jnp.exp(draws), shape[position] // shards_of).reshape((-1,) + (1,) * (len(shape) - position - 1))

    gain = one(*shards[0])
    for cut in shards[1:]:
        gain = gain * one(*cut)
    return gain


def noise(own_key, extent, spread, reach, cuts=(), kind=jnp.bfloat16):
    array = jax.random.normal(own_key, extent, jnp.float32) * spread
    if len(cuts) > 0:
        array = level_of(own_key, extent, cuts, -0.22, 0.18) * array
    return jnp.clip(array, min=-reach, max=reach).astype(kind)


def setup_inputs(seed: int = 0) -> dict:
    keys = jax.random.split(jax.random.key(seed), 7)
    return {
        "hidden_in": noise(keys[0], (N_REP, TOK_REP, D), 1.0, 6.0, ((0, 32), (1, 8))),
        "cotangent": noise(keys[1], (N_REP, TOK_REP, KV_WIDTH), 0.02, 0.119628906, ((0, 32), (1, 8))),
        "token_ids": draw_token_ids(jax.random.fold_in(keys[6], 71), 0),
        "params": noise(keys[3], (N_REP, D, KV_WIDTH), 0.5, 3.0, ((0, 32), (1, 8)), jnp.float32),
        "momentum": noise(keys[4], (N_REP, D, KV_WIDTH), 1.0, 6.0, ((0, 32), (1, 8))),
        "step_index": jax.random.randint(keys[5], (), 0, 64).astype(jnp.int32),
    }


MOMENTUM_DECAY = 0.9
STEP_SIZE = 0.1

def replica_grad(pair):
    xs, gs = pair

    def add_block(total, block):
        part = jnp.dot(block[0].T, block[1], preferred_element_type=jnp.float32)
        rounded = lax.optimization_barrier(part.astype(jnp.bfloat16))
        return (total + rounded.astype(jnp.float32), 0)
    start = jnp.zeros((xs.shape[2], gs.shape[2]), jnp.float32)
    total, unused = lax.scan(add_block, start, (xs, gs))
    return total

def reference(hidden_in, cotangent, token_ids, params, momentum, step_index):
    keep = (token_ids != 0)[..., None]
    masked = jnp.where(keep, cotangent, jnp.zeros_like(cotangent))
    xs = hidden_in.reshape(N_REP, N_SHARD, TOK_DEV, D)
    gs = masked.reshape(N_REP, N_SHARD, TOK_DEV, KV_WIDTH)
    grad = lax.map(replica_grad, (xs, gs))
    hop = (2 ** (step_index % 4)).astype(jnp.int32)
    peer_params = jnp.roll(params, hop, axis=0)
    peer_momentum = jnp.roll(momentum, hop, axis=0)
    mixed_params = 0.5 * (params + peer_params)
    mixed_momentum = 0.5 * (momentum.astype(jnp.float32) + peer_momentum.astype(jnp.float32))
    moment = MOMENTUM_DECAY * mixed_momentum + grad
    new_params = mixed_params - STEP_SIZE * moment
    return (new_params, moment.astype(jnp.bfloat16))
```

```python
from functools import partial

import jax
import jax.numpy as jnp
from jax import lax
from jax.experimental import pallas as pl
from jax.experimental.pallas import tpu as pltpu
from jax.sharding import PartitionSpec as P

MOMENTUM_DECAY = 0.9
STEP_SIZE = 0.1
MESH = pl.DeviceIdType.MESH

N_REP = 32
N_SHARD = 8
RING = 4
TOK = 256
ROWS = 640
WIDTH = 1024
CHUNKS = 5
CHUNK = ROWS // CHUNKS
HALF_TOK = TOK // 2


def step_kernel(
    hop, relay,
    hidden, cotangent, ids, params, momentum, out_params, out_momentum,
    tokens, masked, cot, params32, params16, mom, peer_params, peer_mom, sums_out, sums_in, own,
    load_sem, tok_send, tok_recv, mask_send, mask_recv, gossip_send, gossip_recv, sum_send, sum_recv,
    relay_send, relay_recv, store_sem,
):
    rep, shard = lax.axis_index("rep"), lax.axis_index("shard")
    half, place = shard // RING, shard % RING
    other_half = 1 - half
    across = other_half * RING + place
    ahead, behind = (rep + hop) % N_REP, (rep + N_REP - hop) % N_REP

    def along(distance):
        return (rep, half * RING + (place + distance) % RING)

    def columns(which_half, distance):
        start = (which_half * RING + (place + distance) % RING) * ROWS
        return pl.ds(pl.multiple_of(start, 128), ROWS)

    halves = (other_half, half)
    load_cot = pltpu.make_async_copy(cotangent, cot, load_sem.at[0])
    load_cot.start()
    load_params = pltpu.make_async_copy(params, params32, load_sem.at[1])
    load_params.start()
    load_tok = [
        pltpu.make_async_copy(
            hidden.at[:, columns(halves[kind], 0)], tokens.at[kind, 0], load_sem.at[2 + kind]
        )
        for kind in range(2)
    ]
    load_tok[0].start()
    load_tok[1].start()
    load_mom = pltpu.make_async_copy(momentum, mom, load_sem.at[4])
    load_mom.start()

    sums_to = (behind, across) if relay else (rep, across)
    partners = [along(1), along(2), along(3), (ahead, shard), (behind, shard), sums_to]
    if relay:
        partners.append((ahead, across))
    barrier = pltpu.get_barrier_semaphore()
    for partner in partners:
        pl.semaphore_signal(barrier, inc=1, device_id=partner, device_id_type=MESH)

    load_cot.wait()
    row = lax.broadcasted_iota(jnp.int32, (TOK, TOK), 0)
    col = lax.broadcasted_iota(jnp.int32, (TOK, TOK), 1)
    keep = jnp.logical_and(row == col, jnp.broadcast_to(ids[...], (TOK, TOK)) != 0)
    select = jnp.where(keep, 1.0, 0.0).astype(jnp.bfloat16)
    masked[0] = jnp.dot(select, cot[...], preferred_element_type=jnp.float32).astype(jnp.bfloat16)

    pl.semaphore_wait(barrier, len(partners))

    def remote(src, dst, send, recv, device):
        return pltpu.make_async_remote_copy(
            src_ref=src, dst_ref=dst, send_sem=send, recv_sem=recv,
            device_id=device, device_id_type=MESH,
        )

    send_mask = [
        remote(masked.at[0], masked.at[1], mask_send.at[0], mask_recv.at[0], along(1)),
        remote(masked.at[0], masked.at[3], mask_send.at[1], mask_recv.at[1], along(3)),
    ]
    pass_mask = [
        remote(
            masked.at[1, pl.ds(0, HALF_TOK)], masked.at[2, pl.ds(0, HALF_TOK)],
            mask_send.at[2], mask_recv.at[2], along(1),
        ),
        remote(
            masked.at[3, pl.ds(HALF_TOK, HALF_TOK)], masked.at[2, pl.ds(HALF_TOK, HALF_TOK)],
            mask_send.at[3], mask_recv.at[3], along(3),
        ),
    ]
    send_tok = [
        [
            remote(
                hidden.at[:, columns(halves[kind], distance)], tokens.at[kind, distance],
                tok_send.at[kind, distance - 1], tok_recv.at[kind, distance - 1], along(distance),
            )
            for distance in (1, 3, 2)
        ]
        for kind in range(2)
    ]
    send_params = remote(params16, peer_params, gossip_send.at[0], gossip_recv.at[0], (ahead, shard))
    send_mom = remote(momentum, peer_mom, gossip_send.at[1], gossip_recv.at[1], (ahead, shard))

    for copy in send_mask:
        copy.start()
    for copy in send_tok[0]:
        copy.start()
    load_params.wait()

    @pl.loop(0, CHUNKS)
    def _(c):
        rows = pl.ds(c * CHUNK, CHUNK)
        params16[rows] = params32[rows].astype(jnp.bfloat16)

    send_params.start()
    if not relay:
        send_mom.start()

    send_mask[0].wait_recv()
    pass_mask[0].start()
    send_mask[1].wait_recv()
    pass_mask[1].start()
    for copy in send_tok[0]:
        copy.wait_send()
    for copy in send_tok[1]:
        copy.start()
    for copy in send_tok[0]:
        copy.wait_recv()
    for copy in pass_mask:
        copy.wait_recv()
    load_tok[0].wait()

    def product(kind, c):
        cols = pl.ds(pl.multiple_of(c * CHUNK, CHUNK), CHUNK)
        left = tokens[kind, :, :, cols].reshape(RING * TOK, CHUNK)
        right = masked[...].reshape(RING * TOK, WIDTH)
        return lax.dot_general(left, right, (((0,), (0,)), ((), ())), preferred_element_type=jnp.float32)

    def send_sum(c):
        rows = pl.ds(pl.multiple_of(c * CHUNK, CHUNK), CHUNK)
        return remote(sums_out.at[rows], sums_in.at[rows], sum_send.at[c], sum_recv.at[c], sums_to)

    def send_relay(c):
        rows = pl.ds(pl.multiple_of(c * CHUNK, CHUNK), CHUNK)
        return remote(
            sums_in.at[rows], peer_mom.at[rows], relay_send.at[c], relay_recv.at[c], (ahead, shard)
        )

    @pl.loop(0, CHUNKS)
    def _(c):
        rows = pl.ds(pl.multiple_of(c * CHUNK, CHUNK), CHUNK)
        sums_out[rows] = product(0, c).astype(jnp.bfloat16)
        send_sum(c).start()

    for copy in send_tok[1]:
        copy.wait_recv()
    load_tok[1].wait()
    load_mom.wait()
    share = 0.5 * MOMENTUM_DECAY

    @pl.loop(0, CHUNKS)
    def _(c):
        rows = pl.ds(pl.multiple_of(c * CHUNK, CHUNK), CHUNK)
        own[rows] = product(1, c) + share * mom[rows].astype(jnp.float32)

    if relay:
        @pl.loop(0, CHUNKS)
        def _(c):
            rows = pl.ds(pl.multiple_of(c * CHUNK, CHUNK), CHUNK)
            send_sum(c).wait_recv()
            total = sums_in[rows].astype(jnp.float32) + share * mom[rows].astype(jnp.float32)
            sums_in[rows] = total.astype(jnp.bfloat16)
            send_relay(c).start()

    send_params.wait_recv()
    if not relay:
        send_mom.wait_recv()

    def store(c):
        rows = pl.ds(pl.multiple_of(c * CHUNK, CHUNK), CHUNK)
        return (
            pltpu.make_async_copy(params32.at[rows], out_params.at[rows], store_sem.at[0, c]),
            pltpu.make_async_copy(mom.at[rows], out_momentum.at[rows], store_sem.at[1, c]),
        )

    @pl.loop(0, CHUNKS)
    def _(c):
        rows = pl.ds(pl.multiple_of(c * CHUNK, CHUNK), CHUNK)
        if relay:
            send_relay(c).wait_recv()
            moment = own[rows] + peer_mom[rows].astype(jnp.float32)
        else:
            send_sum(c).wait_recv()
            moment = (
                own[rows] + share * peer_mom[rows].astype(jnp.float32) + sums_in[rows].astype(jnp.float32)
            )
        mixed = 0.5 * (params32[rows] + peer_params[rows].astype(jnp.float32))
        params32[rows] = mixed - STEP_SIZE * moment
        mom[rows] = moment.astype(jnp.bfloat16)
        for copy in store(c):
            copy.start()

    @pl.loop(0, CHUNKS)
    def _(c):
        for copy in store(c):
            copy.wait()
        send_sum(c).wait_send()
        if relay:
            send_relay(c).wait_send()

    send_params.wait_send()
    if not relay:
        send_mom.wait_send()
    for copy in send_mask + pass_mask + send_tok[1]:
        copy.wait_send()


def step_call(hop, relay, collective_id, hidden, cotangent, ids, params, momentum):
    anywhere = pl.BlockSpec(memory_space=pl.ANY)
    bf16, f32, dma = jnp.bfloat16, jnp.float32, pltpu.SemaphoreType.DMA
    return pl.pallas_call(
        partial(step_kernel, hop, relay),
        out_shape=(
            jax.ShapeDtypeStruct((ROWS, WIDTH), f32),
            jax.ShapeDtypeStruct((ROWS, WIDTH), bf16),
        ),
        in_specs=[anywhere, anywhere, pl.BlockSpec(memory_space=pltpu.VMEM), anywhere, anywhere],
        out_specs=(anywhere, anywhere),
        scratch_shapes=[
            pltpu.VMEM((2, RING, TOK, ROWS), bf16),
            pltpu.VMEM((RING, TOK, WIDTH), bf16),
            pltpu.VMEM((TOK, WIDTH), bf16),
            pltpu.VMEM((ROWS, WIDTH), f32),
            pltpu.VMEM((ROWS, WIDTH), bf16),
            pltpu.VMEM((ROWS, WIDTH), bf16),
            pltpu.VMEM((ROWS, WIDTH), bf16),
            pltpu.VMEM((ROWS, WIDTH), bf16),
            pltpu.VMEM((ROWS, WIDTH), bf16),
            pltpu.VMEM((ROWS, WIDTH), bf16),
            pltpu.VMEM((ROWS, WIDTH), f32),
            dma((5,)),
            dma((2, 3)), dma((2, 3)),
            dma((4,)), dma((4,)),
            dma((2,)), dma((2,)),
            dma((CHUNKS,)), dma((CHUNKS,)),
            dma((CHUNKS,)), dma((CHUNKS,)),
            dma((2, CHUNKS)),
        ],
        compiler_params=pltpu.CompilerParams(
            collective_id=collective_id, has_side_effects=True, vmem_limit_bytes=48 * 2**20
        ),
        name=f"step_hop{hop}",
    )(hidden, cotangent, ids, params, momentum)


def on_device(hidden_in, cotangent, token_ids, params, momentum, step_index):
    branches = [partial(step_call, 2**power, power == 2, power) for power in range(4)]
    new_params, new_momentum = lax.switch(
        step_index % 4, branches, hidden_in[0], cotangent[0], token_ids, params[0], momentum[0]
    )
    return (new_params[None], new_momentum[None])


def solution(mesh):
    in_specs = (
        P("rep", "shard", None),
        P("rep", "shard", None),
        P("rep", "shard"),
        P("rep", "shard", None),
        P("rep", "shard", None),
        P(),
    )
    out_specs = (P("rep", "shard", None), P("rep", "shard", None))
    return jax.shard_map(
        on_device, mesh=mesh, in_specs=in_specs, out_specs=out_specs, check_vma=False
    )
```

```python
from functools import partial

import jax
import jax.numpy as jnp
from jax import lax
from jax.experimental import pallas as pl
from jax.experimental.pallas import tpu as pltpu
from jax.sharding import PartitionSpec as P

MOMENTUM_DECAY = 0.9
STEP_SIZE = 0.1
MESH = pl.DeviceIdType.MESH

N_REP = 32
N_SHARD = 8
RING = 4
DEPTH = 8
TOK = 256
ROWS = 640
WIDTH = 1024
CHUNKS = 5
CHUNK = ROWS // CHUNKS
PARTS = 4
PART = WIDTH // PARTS
LAG = 10
SHARE = 0.5 * MOMENTUM_DECAY
FEED = (
    ("mask", 0), ("tok", 0), ("tok", 1), ("mask", 1), ("tok", 2), ("mask", 2), ("tok", 3), ("mask", 3), ("tok", 4),
)


def block_order():
    order, chunks, parts = [], [], []
    for kind, index in FEED:
        if kind == "mask":
            order += [(c, index) for c in chunks]
            parts.append(index)
        else:
            order += [(index, q) for q in parts]
            chunks.append(index)
    return order


def step_kernel(
    hop, routes,
    hidden, cotangent, ids, params, momentum, out_params, out_momentum,
    tokens, turned, own_tokens, masked, cot, params32, params16, mom, peer_params, peer_mom,
    sums, middle, arrived, own,
    load_sem, load_tok_sem, tok_send, tok_recv, own_send, own_recv, mask_send, mask_recv,
    param_send, param_recv, mom_send, mom_recv, first_send, first_recv, second_send, second_recv, store_sem,
):
    order = block_order()
    rep, shard = lax.axis_index("rep"), lax.axis_index("shard")
    half, place = shard // RING, shard % RING
    other_half = 1 - half
    low = (rep // 2) % 4
    across = other_half * RING + place
    ahead, behind = (rep + hop) % N_REP, (rep + N_REP - hop) % N_REP

    def along(distance):
        return (rep, half * RING + (place + distance) % RING)

    def along_z(distance):
        z = (half * 4 + low + distance + DEPTH) % DEPTH
        return ((rep // 8) * 8 + (z % 4) * 2 + rep % 2, (z // 4) * RING + place)

    def columns(which_half, distance, start, size):
        first = (which_half * RING + (place + distance) % RING) * ROWS + start
        return pl.ds(pl.multiple_of(first, 128), size)

    def local(src, dst, sem):
        copy = pltpu.make_async_copy(src, dst, sem)
        copy.start()
        return copy

    load_cot = local(cotangent, cot, load_sem.at[0])
    load_params = local(params, params32, load_sem.at[1])
    load_tok = [
        local(hidden.at[:, columns(other_half, 0, c * CHUNK, CHUNK)], tokens.at[c, 0], load_tok_sem.at[c])
        for c in range(CHUNKS)
    ]
    load_own = local(hidden.at[:, columns(half, 0, 0, ROWS)], own_tokens.at[0], load_sem.at[2])
    load_mom = local(momentum, mom, load_sem.at[3])

    partners = [along(1), along(2), along(3), (ahead, shard), (behind, shard)]
    if "direct" in routes:
        partners.append((rep, across))
    if "relay" in routes:
        partners += [(behind, across), (ahead, across)]
    if "way" in routes:
        partners += [along_z(2), along_z(-2)]
    barrier = pltpu.get_barrier_semaphore()
    for partner in partners:
        pl.semaphore_signal(barrier, inc=1, device_id=partner, device_id_type=MESH)

    first_to = {
        "direct": (rep, across),
        "relay": (behind, across),
        "way": along_z(jnp.where(low >= 1, -2, 2)),
    }
    second_to = {"relay": (ahead, shard), "way": along_z(jnp.where(low == 2, 2, -2))}

    load_cot.wait()
    row = lax.broadcasted_iota(jnp.int32, (TOK, TOK), 0)
    col = lax.broadcasted_iota(jnp.int32, (TOK, TOK), 1)
    keep = jnp.logical_and(row == col, jnp.broadcast_to(ids[...], (TOK, TOK)) != 0)
    select = jnp.where(keep, 1.0, 0.0).astype(jnp.bfloat16)
    for q in range(PARTS):
        masked[q, 0] = jnp.dot(
            select, cot[:, q * PART:(q + 1) * PART], preferred_element_type=jnp.float32
        ).astype(jnp.bfloat16)

    pl.semaphore_wait(barrier, len(partners))

    def remote(src, dst, send, recv, device):
        return pltpu.make_async_remote_copy(
            src_ref=src, dst_ref=dst, send_sem=send, recv_sem=recv,
            device_id=device, device_id_type=MESH,
        )

    feed = {}
    for kind, index in FEED:
        feed[kind, index] = []
        for d in (1, 3, 2):
            if kind == "mask":
                copy = remote(
                    masked.at[index, 0], masked.at[index, d],
                    mask_send.at[index, d - 1], mask_recv.at[index, d - 1], along(d),
                )
            else:
                copy = remote(
                    hidden.at[:, columns(other_half, d, index * CHUNK, CHUNK)], tokens.at[index, d],
                    tok_send.at[index, d - 1], tok_recv.at[index, d - 1], along(d),
                )
            copy.start()
            feed[kind, index].append(copy)

    send_mom = []
    for q in range(PARTS):
        if routes[q] != "relay":
            cols = pl.ds(q * PART, PART)
            copy = remote(
                momentum.at[:, cols], peer_mom.at[:, cols], mom_send.at[q], mom_recv.at[q], (ahead, shard)
            )
            copy.start()
            send_mom.append(copy)

    load_params.wait()

    @pl.loop(0, CHUNKS)
    def _(c):
        rows = pl.ds(pl.multiple_of(c * CHUNK, CHUNK), CHUNK)
        params16[rows] = params32[rows].astype(jnp.bfloat16)

    send_params = remote(params16, peer_params, param_send.at[0], param_recv.at[0], (ahead, shard))
    send_params.start()

    send_own = [
        remote(
            hidden.at[:, columns(half, d, 0, ROWS)], own_tokens.at[d], own_send.at[d - 1], own_recv.at[d - 1], along(d)
        )
        for d in (1, 3, 2)
    ]
    for copy in send_own:
        copy.start()
    load_mom.wait()

    def block(c, q):
        return (pl.ds(c * CHUNK, CHUNK), pl.ds(q * PART, PART))

    def first_leg(c, q):
        at, i = block(c, q), c * PARTS + q
        landing = arrived if routes[q] == "direct" else middle
        return remote(sums.at[at], landing.at[at], first_send.at[i], first_recv.at[i], first_to[routes[q]])

    def second_leg(c, q):
        at, i = block(c, q), c * PARTS + q
        return remote(middle.at[at], arrived.at[at], second_send.at[i], second_recv.at[i], second_to[routes[q]])

    first, second, have = {}, {}, set()

    def pass_on(c, q):
        if routes[q] == "direct":
            return
        at = block(c, q)
        first[c, q].wait_recv()
        if routes[q] == "relay":
            middle[at] = (middle[at].astype(jnp.float32) + SHARE * mom[at].astype(jnp.float32)).astype(jnp.bfloat16)
        second[c, q] = second_leg(c, q)
        second[c, q].start()

    def need(kind, index):
        if (kind, index) in have:
            return
        have.add((kind, index))
        for copy in feed[kind, index]:
            copy.wait_recv()
        if kind == "tok":
            load_tok[index].wait()
            turned[index] = tokens[index].reshape(RING * TOK, CHUNK).T

    for i, (c, q) in enumerate(order):
        need("mask", q)
        need("tok", c)
        at = block(c, q)
        sums[at] = jnp.dot(
            turned[c], masked[q].reshape(RING * TOK, PART), preferred_element_type=jnp.float32
        ).astype(jnp.bfloat16)
        first[c, q] = first_leg(c, q)
        first[c, q].start()
        if i >= LAG:
            pass_on(*order[i - LAG])

    for copy in send_own:
        copy.wait_recv()
    load_own.wait()

    @pl.loop(0, CHUNKS)
    def _(c):
        rows = pl.ds(pl.multiple_of(c * CHUNK, CHUNK), CHUNK)
        left = own_tokens[:, :, rows].reshape(RING * TOK, CHUNK).T
        for q in range(PARTS):
            cols = pl.ds(q * PART, PART)
            own[rows, cols] = jnp.dot(
                left, masked[q].reshape(RING * TOK, PART), preferred_element_type=jnp.float32
            ) + SHARE * mom[rows, cols].astype(jnp.float32)

    for c, q in order[len(order) - LAG:]:
        pass_on(c, q)

    send_params.wait_recv()
    for copy in send_mom:
        copy.wait_recv()
    stores = []
    for c, q in order:
        at, i = block(c, q), c * PARTS + q
        if routes[q] == "direct":
            first[c, q].wait_recv()
        else:
            second[c, q].wait_recv()
        moment = own[at] + arrived[at].astype(jnp.float32)
        if routes[q] != "relay":
            moment = moment + SHARE * peer_mom[at].astype(jnp.float32)
        mixed = 0.5 * (params32[at] + peer_params[at].astype(jnp.float32))
        params32[at] = mixed - STEP_SIZE * moment
        mom[at] = moment.astype(jnp.bfloat16)
        stores.append(local(params32.at[at], out_params.at[at], store_sem.at[0, i]))
        stores.append(local(mom.at[at], out_momentum.at[at], store_sem.at[1, i]))

    for copies in feed.values():
        for copy in copies:
            copy.wait_send()
    for copy in send_own + send_mom + [send_params] + list(first.values()) + list(second.values()):
        copy.wait_send()
    for copy in stores:
        copy.wait()


def step_call(power, hidden, cotangent, ids, params, momentum):
    hop = 2**power
    anywhere = pl.BlockSpec(memory_space=pl.ANY)
    bf16, f32, dma = jnp.bfloat16, jnp.float32, pltpu.SemaphoreType.DMA
    blocks = CHUNKS * PARTS
    return pl.pallas_call(
        partial(step_kernel, hop, ROUTES[power]),
        out_shape=(
            jax.ShapeDtypeStruct((ROWS, WIDTH), f32),
            jax.ShapeDtypeStruct((ROWS, WIDTH), bf16),
        ),
        in_specs=[anywhere, anywhere, pl.BlockSpec(memory_space=pltpu.VMEM), anywhere, anywhere],
        out_specs=(anywhere, anywhere),
        scratch_shapes=[
            pltpu.VMEM((CHUNKS, RING, TOK, CHUNK), bf16),
            pltpu.VMEM((CHUNKS, CHUNK, RING * TOK), bf16),
            pltpu.VMEM((RING, TOK, ROWS), bf16),
            pltpu.VMEM((PARTS, RING, TOK, PART), bf16),
            pltpu.VMEM((TOK, WIDTH), bf16),
            pltpu.VMEM((ROWS, WIDTH), f32),
            pltpu.VMEM((ROWS, WIDTH), bf16),
            pltpu.VMEM((ROWS, WIDTH), bf16),
            pltpu.VMEM((ROWS, WIDTH), bf16),
            pltpu.VMEM((ROWS, WIDTH), bf16),
            pltpu.VMEM((ROWS, WIDTH), bf16),
            pltpu.VMEM((ROWS, WIDTH), bf16),
            pltpu.VMEM((ROWS, WIDTH), bf16),
            pltpu.VMEM((ROWS, WIDTH), f32),
            dma((4,)), dma((CHUNKS,)),
            dma((CHUNKS, 3)), dma((CHUNKS, 3)),
            dma((3,)), dma((3,)),
            dma((PARTS, 3)), dma((PARTS, 3)),
            dma((1,)), dma((1,)),
            dma((PARTS,)), dma((PARTS,)),
            dma((blocks,)), dma((blocks,)),
            dma((blocks,)), dma((blocks,)),
            dma((2, blocks)),
        ],
        compiler_params=pltpu.CompilerParams(
            collective_id=power, has_side_effects=True, vmem_limit_bytes=48 * 2**20
        ),
        name=f"step_hop{hop}",
    )(hidden, cotangent, ids, params, momentum)


ROUTES = (
    ("direct",) * 4,
    ("relay", "way", "relay", "way"),
    ("relay",) * 4,
    ("direct",) * 4,
)


def on_device(hidden_in, cotangent, token_ids, params, momentum, step_index):
    branches = [partial(step_call, power) for power in range(4)]
    new_params, new_momentum = lax.switch(
        step_index % 4, branches, hidden_in[0], cotangent[0], token_ids, params[0], momentum[0]
    )
    return (new_params[None], new_momentum[None])


def solution(mesh):
    in_specs = (
        P("rep", "shard", None),
        P("rep", "shard", None),
        P("rep", "shard"),
        P("rep", "shard", None),
        P("rep", "shard", None),
        P(),
    )
    out_specs = (P("rep", "shard", None), P("rep", "shard", None))
    return jax.shard_map(
        on_device, mesh=mesh, in_specs=in_specs, out_specs=out_specs, check_vma=False
    )
```

```python
from functools import partial

import jax
import jax.numpy as jnp
from jax import lax
from jax.experimental import pallas as pl
from jax.experimental.pallas import tpu as pltpu
from jax.sharding import PartitionSpec as P

MOMENTUM_DECAY = 0.9
STEP_SIZE = 0.1
MESH = pl.DeviceIdType.MESH

N_REP = 32
N_SHARD = 8
RING = 4
DEPTH = 8
TOK = 256
ROWS = 640
WIDTH = 1024
CHUNKS = 5
CHUNK = ROWS // CHUNKS
PARTS = 4
PART = WIDTH // PARTS
LAG = 10
SHARE = 0.5 * MOMENTUM_DECAY
FEED = (
    ("mask", 0), ("tok", 0), ("tok", 1), ("mask", 1), ("tok", 2), ("mask", 2), ("tok", 3), ("mask", 3), ("tok", 4),
)


def block_order():
    order, chunks, parts = [], [], []
    for kind, index in FEED:
        if kind == "mask":
            order += [(c, index) for c in chunks]
            parts.append(index)
        else:
            order += [(index, q) for q in parts]
            chunks.append(index)
    return order


def step_kernel(
    hop, route,
    hidden, cotangent, ids, params, momentum, out_params, out_momentum,
    tokens, turned, own_tokens, masked, cot, params32, params16, mom, peer_params, peer_mom,
    sums, middle, halfway, arrived, own,
    load_sem, load_tok_sem, tok_send, tok_recv, own_send, own_recv, mask_send, mask_recv,
    param_send, param_recv, mom_send, mom_recv, first_send, first_recv, second_send, second_recv,
    way_recv, way_send, store_sem,
):
    order = block_order()
    rep, shard = lax.axis_index("rep"), lax.axis_index("shard")
    half, place = shard // RING, shard % RING
    other_half = 1 - half
    low = (rep // 2) % 4
    across = other_half * RING + place
    ahead, behind = (rep + hop) % N_REP, (rep + N_REP - hop) % N_REP

    def along(distance):
        return (rep, half * RING + (place + distance) % RING)

    def along_z(distance):
        z = (half * 4 + low + distance + DEPTH) % DEPTH
        return ((rep // 8) * 8 + (z % 4) * 2 + rep % 2, (z // 4) * RING + place)

    def columns(which_half, distance, start, size):
        first = (which_half * RING + (place + distance) % RING) * ROWS + start
        return pl.ds(pl.multiple_of(first, 128), size)

    def local(src, dst, sem):
        copy = pltpu.make_async_copy(src, dst, sem)
        copy.start()
        return copy

    load_cot = local(cotangent, cot, load_sem.at[0])
    load_params = local(params, params32, load_sem.at[1])
    load_tok = [
        local(hidden.at[:, columns(other_half, 0, c * CHUNK, CHUNK)], tokens.at[c, 0], load_tok_sem.at[c])
        for c in range(CHUNKS)
    ]
    load_own = local(hidden.at[:, columns(half, 0, 0, ROWS)], own_tokens.at[0], load_sem.at[2])
    load_mom = local(momentum, mom, load_sem.at[3])

    def where(test, run):
        if isinstance(test, bool):
            if test:
                run()
        else:
            pl.when(test)(run)

    direct = route == "direct"
    always = route == "relay"

    def relayed(c, replica):
        if direct or always:
            return always
        if route == "even":
            return replica % 2 == 0
        return c % 2 == 0 or (replica // 2) % 4 == 0

    def otherwise(test):
        return not test if isinstance(test, bool) else jnp.logical_not(test)

    partners = [along(1), along(2), along(3), (ahead, shard), (behind, shard)]
    if direct:
        partners.append((rep, across))
    else:
        partners += [(behind, across), (ahead, across)]
        if not always:
            partners += [along_z(2), along_z(-2)]
    barrier = pltpu.get_barrier_semaphore()
    for partner in partners:
        pl.semaphore_signal(barrier, inc=1, device_id=partner, device_id_type=MESH)

    relay_first, relay_second = (behind, across), (ahead, shard)
    way_first = along_z(jnp.where(low >= 1, -2, 2))
    way_second = along_z(jnp.where(low == 2, 2, -2))
    way_rep = way_second[0]

    load_cot.wait()
    row = lax.broadcasted_iota(jnp.int32, (TOK, TOK), 0)
    col = lax.broadcasted_iota(jnp.int32, (TOK, TOK), 1)
    keep = jnp.logical_and(row == col, jnp.broadcast_to(ids[...], (TOK, TOK)) != 0)
    select = jnp.where(keep, 1.0, 0.0).astype(jnp.bfloat16)
    for q in range(PARTS):
        masked[q, 0] = jnp.dot(
            select, cot[:, q * PART:(q + 1) * PART], preferred_element_type=jnp.float32
        ).astype(jnp.bfloat16)

    pl.semaphore_wait(barrier, len(partners))

    def remote(src, dst, send, recv, device):
        return pltpu.make_async_remote_copy(
            src_ref=src, dst_ref=dst, send_sem=send, recv_sem=recv,
            device_id=device, device_id_type=MESH,
        )

    feed = {}
    for kind, index in FEED:
        feed[kind, index] = []
        for d in (1, 3, 2):
            if kind == "mask":
                copy = remote(
                    masked.at[index, 0], masked.at[index, d],
                    mask_send.at[index, d - 1], mask_recv.at[index, d - 1], along(d),
                )
            else:
                copy = remote(
                    hidden.at[:, columns(other_half, d, index * CHUNK, CHUNK)], tokens.at[index, d],
                    tok_send.at[index, d - 1], tok_recv.at[index, d - 1], along(d),
                )
            copy.start()
            feed[kind, index].append(copy)

    def send_mom(c):
        rows = pl.ds(c * CHUNK, CHUNK)
        return remote(momentum.at[rows], peer_mom.at[rows], mom_send.at[c], mom_recv.at[c], (ahead, shard))

    for c in range(CHUNKS):
        where(otherwise(relayed(c, ahead)), send_mom(c).start)

    load_params.wait()

    @pl.loop(0, CHUNKS)
    def _(c):
        rows = pl.ds(pl.multiple_of(c * CHUNK, CHUNK), CHUNK)
        params16[rows] = params32[rows].astype(jnp.bfloat16)

    send_params = remote(params16, peer_params, param_send.at[0], param_recv.at[0], (ahead, shard))
    send_params.start()

    send_own = [
        remote(
            hidden.at[:, columns(half, d, 0, ROWS)], own_tokens.at[d], own_send.at[d - 1], own_recv.at[d - 1], along(d)
        )
        for d in (1, 3, 2)
    ]
    for copy in send_own:
        copy.start()
    load_mom.wait()

    def block(c, q):
        return (pl.ds(c * CHUNK, CHUNK), pl.ds(q * PART, PART))

    def number(c, q):
        return c * PARTS + q

    def straight(c, q):
        at, i = block(c, q), number(c, q)
        return remote(sums.at[at], arrived.at[at], first_send.at[i], first_recv.at[i], (rep, across))

    def relay_leg(c, q):
        at, i = block(c, q), number(c, q)
        return remote(sums.at[at], middle.at[at], first_send.at[i], first_recv.at[i], relay_first)

    def way_leg(c, q):
        at, i = block(c, q), number(c, q)
        return remote(sums.at[at], halfway.at[at], first_send.at[i], way_recv.at[i], way_first)

    def relay_last(c, q):
        at, i = block(c, q), number(c, q)
        return remote(middle.at[at], arrived.at[at], second_send.at[i], second_recv.at[i], relay_second)

    def way_last(c, q):
        at, i = block(c, q), number(c, q)
        return remote(halfway.at[at], arrived.at[at], way_send.at[i], second_recv.at[i], way_second)

    def leave(c, q):
        if direct:
            straight(c, q).start()
        else:
            where(relayed(c, rep), relay_leg(c, q).start)
            where(otherwise(relayed(c, rep)), way_leg(c, q).start)

    have = set()

    def pass_on(c, q):
        if direct:
            return
        at = block(c, q)

        def relay():
            relay_leg(c, q).wait_recv()
            middle[at] = (middle[at].astype(jnp.float32) + SHARE * mom[at].astype(jnp.float32)).astype(jnp.bfloat16)
            relay_last(c, q).start()

        def way():
            way_leg(c, q).wait_recv()
            way_last(c, q).start()

        where(otherwise(relayed(c, way_rep)), way)
        where(relayed(c, ahead), relay)

    def need(kind, index):
        if (kind, index) in have:
            return
        have.add((kind, index))
        for copy in feed[kind, index]:
            copy.wait_recv()
        if kind == "tok":
            load_tok[index].wait()
            turned[index] = tokens[index].reshape(RING * TOK, CHUNK).T

    for i, (c, q) in enumerate(order):
        need("mask", q)
        need("tok", c)
        at = block(c, q)
        sums[at] = jnp.dot(
            turned[c], masked[q].reshape(RING * TOK, PART), preferred_element_type=jnp.float32
        ).astype(jnp.bfloat16)
        leave(c, q)
        if i >= LAG:
            pass_on(*order[i - LAG])

    for copy in send_own:
        copy.wait_recv()
    load_own.wait()

    @pl.loop(0, CHUNKS)
    def _(c):
        rows = pl.ds(pl.multiple_of(c * CHUNK, CHUNK), CHUNK)
        left = own_tokens[:, :, rows].reshape(RING * TOK, CHUNK).T
        for q in range(PARTS):
            cols = pl.ds(q * PART, PART)
            own[rows, cols] = jnp.dot(
                left, masked[q].reshape(RING * TOK, PART), preferred_element_type=jnp.float32
            ) + SHARE * mom[rows, cols].astype(jnp.float32)

    for c, q in order[len(order) - LAG:]:
        pass_on(c, q)

    send_params.wait_recv()

    for c in range(CHUNKS):
        def add_peer(c=c):
            rows = pl.ds(c * CHUNK, CHUNK)
            send_mom(c).wait_recv()
            own[rows] = own[rows] + SHARE * peer_mom[rows].astype(jnp.float32)

        where(otherwise(relayed(c, rep)), add_peer)
    stores = []
    for c, q in order:
        at, i = block(c, q), number(c, q)
        if direct:
            straight(c, q).wait_recv()
        else:
            relay_last(c, q).wait_recv()
        moment = own[at] + arrived[at].astype(jnp.float32)
        mixed = 0.5 * (params32[at] + peer_params[at].astype(jnp.float32))
        params32[at] = mixed - STEP_SIZE * moment
        mom[at] = moment.astype(jnp.bfloat16)
        stores.append(local(params32.at[at], out_params.at[at], store_sem.at[0, i]))
        stores.append(local(mom.at[at], out_momentum.at[at], store_sem.at[1, i]))

    for copies in feed.values():
        for copy in copies:
            copy.wait_send()
    for copy in send_own + [send_params]:
        copy.wait_send()
    for c in range(CHUNKS):
        where(otherwise(relayed(c, ahead)), send_mom(c).wait_send)
    for c, q in order:
        straight(c, q).wait_send()
        if not direct:
            where(relayed(c, ahead), relay_last(c, q).wait_send)
            where(otherwise(relayed(c, way_rep)), way_last(c, q).wait_send)
    for copy in stores:
        copy.wait()


def step_call(power, hidden, cotangent, ids, params, momentum):
    hop = 2**power
    anywhere = pl.BlockSpec(memory_space=pl.ANY)
    bf16, f32, dma = jnp.bfloat16, jnp.float32, pltpu.SemaphoreType.DMA
    blocks = CHUNKS * PARTS
    return pl.pallas_call(
        partial(step_kernel, hop, ROUTES[power]),
        out_shape=(
            jax.ShapeDtypeStruct((ROWS, WIDTH), f32),
            jax.ShapeDtypeStruct((ROWS, WIDTH), bf16),
        ),
        in_specs=[anywhere, anywhere, pl.BlockSpec(memory_space=pltpu.VMEM), anywhere, anywhere],
        out_specs=(anywhere, anywhere),
        scratch_shapes=[
            pltpu.VMEM((CHUNKS, RING, TOK, CHUNK), bf16),
            pltpu.VMEM((CHUNKS, CHUNK, RING * TOK), bf16),
            pltpu.VMEM((RING, TOK, ROWS), bf16),
            pltpu.VMEM((PARTS, RING, TOK, PART), bf16),
            pltpu.VMEM((TOK, WIDTH), bf16),
            pltpu.VMEM((ROWS, WIDTH), f32),
            pltpu.VMEM((ROWS, WIDTH), bf16),
            pltpu.VMEM((ROWS, WIDTH), bf16),
            pltpu.VMEM((ROWS, WIDTH), bf16),
            pltpu.VMEM((ROWS, WIDTH), bf16),
            pltpu.VMEM((ROWS, WIDTH), bf16),
            pltpu.VMEM((ROWS, WIDTH), bf16),
            pltpu.VMEM((ROWS, WIDTH), bf16),
            pltpu.VMEM((ROWS, WIDTH), bf16),
            pltpu.VMEM((ROWS, WIDTH), f32),
            dma((4,)), dma((CHUNKS,)),
            dma((CHUNKS, 3)), dma((CHUNKS, 3)),
            dma((3,)), dma((3,)),
            dma((PARTS, 3)), dma((PARTS, 3)),
            dma((1,)), dma((1,)),
            dma((CHUNKS,)), dma((CHUNKS,)),
            dma((blocks,)), dma((blocks,)),
            dma((blocks,)), dma((blocks,)),
            dma((blocks,)), dma((blocks,)),
            dma((2, blocks)),
        ],
        compiler_params=pltpu.CompilerParams(
            collective_id=power, has_side_effects=True, vmem_limit_bytes=48 * 2**20
        ),
        name=f"step_hop{hop}",
    )(hidden, cotangent, ids, params, momentum)


ROUTES = ("even", "mixed", "relay", "direct")


def on_device(hidden_in, cotangent, token_ids, params, momentum, step_index):
    branches = [partial(step_call, power) for power in range(4)]
    new_params, new_momentum = lax.switch(
        step_index % 4, branches, hidden_in[0], cotangent[0], token_ids, params[0], momentum[0]
    )
    return (new_params[None], new_momentum[None])


def solution(mesh):
    in_specs = (
        P("rep", "shard", None),
        P("rep", "shard", None),
        P("rep", "shard"),
        P("rep", "shard", None),
        P("rep", "shard", None),
        P(),
    )
    out_specs = (P("rep", "shard", None), P("rep", "shard", None))
    return jax.shard_map(
        on_device, mesh=mesh, in_specs=in_specs, out_specs=out_specs, check_vma=False
    )
```

```python
from functools import partial

import jax
import jax.numpy as jnp
from jax import lax
from jax.experimental import pallas as pl
from jax.experimental.pallas import tpu as pltpu
from jax.sharding import PartitionSpec as P

MOMENTUM_DECAY = 0.9
STEP_SIZE = 0.1
MESH = pl.DeviceIdType.MESH

N_REP = 32
N_SHARD = 8
RING = 4
DEPTH = 8
TOK = 256
ROWS = 640
WIDTH = 1024
CHUNKS = 5
CHUNK = ROWS // CHUNKS
PARTS = 4
PART = WIDTH // PARTS
SHARE = 0.5 * MOMENTUM_DECAY
FEED = (
    ("mask", 0), ("tok", 0), ("tok", 1), ("mask", 1), ("tok", 2), ("mask", 2), ("tok", 3), ("mask", 3), ("tok", 4),
)


def block_order():
    order, chunks, parts = [], [], []
    for kind, index in FEED:
        if kind == "mask":
            order += [(c, index) for c in chunks]
            parts.append(index)
        else:
            order += [(index, q) for q in parts]
            chunks.append(index)
    return order


def step_kernel(
    hop, route, lags, late,
    hidden, cotangent, ids, params, momentum, out_params, out_momentum,
    tokens, turned, own_tokens, masked, cot, params32, params16, mom, peer_params, peer_mom,
    sums, middle, halfway, arrived, own,
    load_sem, load_tok_sem, tok_send, tok_recv, own_send, own_recv, mask_send, mask_recv,
    param_send, param_recv, mom_send, mom_recv, first_send, first_recv, second_send, second_recv,
    way_recv, way_send, store_sem,
):
    order = block_order()
    rep, shard = lax.axis_index("rep"), lax.axis_index("shard")
    half, place = shard // RING, shard % RING
    other_half = 1 - half
    low = (rep // 2) % 4
    across = other_half * RING + place
    ahead, behind = (rep + hop) % N_REP, (rep + N_REP - hop) % N_REP

    def along(distance):
        return (rep, half * RING + (place + distance) % RING)

    def along_z(distance):
        z = (half * 4 + low + distance + DEPTH) % DEPTH
        return ((rep // 8) * 8 + (z % 4) * 2 + rep % 2, (z // 4) * RING + place)

    def columns(which_half, distance, start, size):
        first = (which_half * RING + (place + distance) % RING) * ROWS + start
        return pl.ds(pl.multiple_of(first, 128), size)

    def local(src, dst, sem):
        copy = pltpu.make_async_copy(src, dst, sem)
        copy.start()
        return copy

    load_cot = local(cotangent, cot, load_sem.at[0])
    load_params = local(params, params32, load_sem.at[1])
    load_tok = [
        local(hidden.at[:, columns(other_half, 0, c * CHUNK, CHUNK)], tokens.at[c, 0], load_tok_sem.at[c])
        for c in range(CHUNKS)
    ]
    load_own = local(hidden.at[:, columns(half, 0, 0, ROWS)], own_tokens.at[0], load_sem.at[2])
    load_mom = local(momentum, mom, load_sem.at[3])

    def where(test, run):
        if isinstance(test, bool):
            if test:
                run()
        else:
            pl.when(test)(run)

    direct = route == "direct"
    always = route == "relay"

    def relayed(c, replica):
        if direct or always:
            return always
        if route == "even":
            return replica % 2 == 0
        return c % 2 == 0 or (replica // 2) % 4 == 0

    def otherwise(test):
        return not test if isinstance(test, bool) else jnp.logical_not(test)

    partners = [along(1), along(2), along(3), (ahead, shard), (behind, shard)]
    if direct:
        partners.append((rep, across))
    else:
        partners += [(behind, across), (ahead, across)]
        if not always:
            partners += [along_z(2), along_z(-2)]
    barrier = pltpu.get_barrier_semaphore()
    for partner in partners:
        pl.semaphore_signal(barrier, inc=1, device_id=partner, device_id_type=MESH)

    relay_first, relay_second = (behind, across), (ahead, shard)
    way_first = along_z(jnp.where(low >= 1, -2, 2))
    way_second = along_z(jnp.where(low == 2, 2, -2))
    way_rep = way_second[0]

    load_cot.wait()
    row = lax.broadcasted_iota(jnp.int32, (TOK, TOK), 0)
    col = lax.broadcasted_iota(jnp.int32, (TOK, TOK), 1)
    keep = jnp.logical_and(row == col, jnp.broadcast_to(ids[...], (TOK, TOK)) != 0)
    select = jnp.where(keep, 1.0, 0.0).astype(jnp.bfloat16)
    for q in range(PARTS):
        masked[q, 0] = jnp.dot(
            select, cot[:, q * PART:(q + 1) * PART], preferred_element_type=jnp.float32
        ).astype(jnp.bfloat16)

    load_params.wait()

    @pl.loop(0, CHUNKS)
    def _(c):
        rows = pl.ds(pl.multiple_of(c * CHUNK, CHUNK), CHUNK)
        params16[rows] = params32[rows].astype(jnp.bfloat16)

    pl.semaphore_wait(barrier, len(partners))

    def remote(src, dst, send, recv, device):
        return pltpu.make_async_remote_copy(
            src_ref=src, dst_ref=dst, send_sem=send, recv_sem=recv,
            device_id=device, device_id_type=MESH,
        )

    feed = {}

    def give(kind, index):
        feed[kind, index] = []
        for d in (1, 3, 2):
            if kind == "mask":
                copy = remote(
                    masked.at[index, 0], masked.at[index, d],
                    mask_send.at[index, d - 1], mask_recv.at[index, d - 1], along(d),
                )
            else:
                copy = remote(
                    hidden.at[:, columns(other_half, d, index * CHUNK, CHUNK)], tokens.at[index, d],
                    tok_send.at[index, d - 1], tok_recv.at[index, d - 1], along(d),
                )
            copy.start()
            feed[kind, index].append(copy)

    for item in FEED[:2]:
        give(*item)

    send_params = remote(params16, peer_params, param_send.at[0], param_recv.at[0], (ahead, shard))
    send_params.start()

    def send_mom(c):
        rows = pl.ds(c * CHUNK, CHUNK)
        return remote(momentum.at[rows], peer_mom.at[rows], mom_send.at[c], mom_recv.at[c], (ahead, shard))

    for c in range(CHUNKS):
        where(otherwise(relayed(c, ahead)), send_mom(c).start)

    for item in FEED[2:]:
        give(*item)

    send_own = [
        remote(
            hidden.at[:, columns(half, d, 0, ROWS)], own_tokens.at[d], own_send.at[d - 1], own_recv.at[d - 1], along(d)
        )
        for d in (1, 3, 2)
    ]
    for copy in send_own:
        copy.start()
    load_mom.wait()

    def block(c, q):
        return (pl.ds(c * CHUNK, CHUNK), pl.ds(q * PART, PART))

    def number(c, q):
        return c * PARTS + q

    def straight(c, q):
        at, i = block(c, q), number(c, q)
        return remote(sums.at[at], arrived.at[at], first_send.at[i], first_recv.at[i], (rep, across))

    def relay_leg(c, q):
        at, i = block(c, q), number(c, q)
        return remote(sums.at[at], middle.at[at], first_send.at[i], first_recv.at[i], relay_first)

    def way_leg(c, q):
        at, i = block(c, q), number(c, q)
        return remote(sums.at[at], halfway.at[at], first_send.at[i], way_recv.at[i], way_first)

    def relay_last(c, q):
        at, i = block(c, q), number(c, q)
        return remote(middle.at[at], arrived.at[at], second_send.at[i], second_recv.at[i], relay_second)

    def way_last(c, q):
        at, i = block(c, q), number(c, q)
        return remote(halfway.at[at], arrived.at[at], way_send.at[i], second_recv.at[i], way_second)

    def leave(c, q):
        if direct:
            straight(c, q).start()
        else:
            where(relayed(c, rep), relay_leg(c, q).start)
            where(otherwise(relayed(c, rep)), way_leg(c, q).start)

    have = set()

    def pass_relay(c, q):
        def run():
            at = block(c, q)
            relay_leg(c, q).wait_recv()
            middle[at] = (middle[at].astype(jnp.float32) + SHARE * mom[at].astype(jnp.float32)).astype(jnp.bfloat16)
            relay_last(c, q).start()

        where(relayed(c, ahead), run)

    def pass_way(c, q):
        def run():
            way_leg(c, q).wait_recv()
            way_last(c, q).start()

        where(otherwise(relayed(c, way_rep)), run)

    passed = [0, 0]

    def pass_until(*limits):
        if direct:
            return
        for i in range(len(order)):
            for k, run in enumerate((pass_way, pass_relay)):
                if passed[k] == i and i < limits[k]:
                    run(*order[i])
                    passed[k] = i + 1

    def need(kind, index):
        if (kind, index) in have:
            return
        have.add((kind, index))
        for copy in feed[kind, index]:
            copy.wait_recv()
        if kind == "tok":
            load_tok[index].wait()
            turned[index] = tokens[index].reshape(RING * TOK, CHUNK).T

    for i, (c, q) in enumerate(order):
        need("mask", q)
        need("tok", c)
        at = block(c, q)
        sums[at] = jnp.dot(
            turned[c], masked[q].reshape(RING * TOK, PART), preferred_element_type=jnp.float32
        ).astype(jnp.bfloat16)
        leave(c, q)
        pass_until(i + 1 - lags[0], i + 1 - lags[1])

    pass_until(len(order) - late, len(order) - late)

    for copy in send_own:
        copy.wait_recv()
    load_own.wait()

    @pl.loop(0, CHUNKS)
    def _(c):
        rows = pl.ds(pl.multiple_of(c * CHUNK, CHUNK), CHUNK)
        left = own_tokens[:, :, rows].reshape(RING * TOK, CHUNK).T
        for q in range(PARTS):
            cols = pl.ds(q * PART, PART)
            own[rows, cols] = jnp.dot(
                left, masked[q].reshape(RING * TOK, PART), preferred_element_type=jnp.float32
            ) + SHARE * mom[rows, cols].astype(jnp.float32)

    pass_until(len(order), len(order))

    send_params.wait_recv()

    for c in range(CHUNKS):
        def add_peer(c=c):
            rows = pl.ds(c * CHUNK, CHUNK)
            send_mom(c).wait_recv()
            own[rows] = own[rows] + SHARE * peer_mom[rows].astype(jnp.float32)

        where(otherwise(relayed(c, rep)), add_peer)
    stores = []
    for c, q in order:
        at, i = block(c, q), number(c, q)
        if direct:
            straight(c, q).wait_recv()
        else:
            relay_last(c, q).wait_recv()
        moment = own[at] + arrived[at].astype(jnp.float32)
        mixed = 0.5 * (params32[at] + peer_params[at].astype(jnp.float32))
        params32[at] = mixed - STEP_SIZE * moment
        mom[at] = moment.astype(jnp.bfloat16)
        stores.append(local(params32.at[at], out_params.at[at], store_sem.at[0, i]))
        stores.append(local(mom.at[at], out_momentum.at[at], store_sem.at[1, i]))

    for copies in feed.values():
        for copy in copies:
            copy.wait_send()
    for copy in send_own + [send_params]:
        copy.wait_send()
    for c in range(CHUNKS):
        where(otherwise(relayed(c, ahead)), send_mom(c).wait_send)
    for c, q in order:
        straight(c, q).wait_send()
        if not direct:
            where(relayed(c, ahead), relay_last(c, q).wait_send)
            where(otherwise(relayed(c, way_rep)), way_last(c, q).wait_send)
    for copy in stores:
        copy.wait()


def step_call(power, hidden, cotangent, ids, params, momentum):
    hop = 2**power
    anywhere = pl.BlockSpec(memory_space=pl.ANY)
    bf16, f32, dma = jnp.bfloat16, jnp.float32, pltpu.SemaphoreType.DMA
    blocks = CHUNKS * PARTS
    return pl.pallas_call(
        partial(step_kernel, hop, *PLANS[power]),
        out_shape=(
            jax.ShapeDtypeStruct((ROWS, WIDTH), f32),
            jax.ShapeDtypeStruct((ROWS, WIDTH), bf16),
        ),
        in_specs=[anywhere, anywhere, pl.BlockSpec(memory_space=pltpu.VMEM), anywhere, anywhere],
        out_specs=(anywhere, anywhere),
        scratch_shapes=[
            pltpu.VMEM((CHUNKS, RING, TOK, CHUNK), bf16),
            pltpu.VMEM((CHUNKS, CHUNK, RING * TOK), bf16),
            pltpu.VMEM((RING, TOK, ROWS), bf16),
            pltpu.VMEM((PARTS, RING, TOK, PART), bf16),
            pltpu.VMEM((TOK, WIDTH), bf16),
            pltpu.VMEM((ROWS, WIDTH), f32),
            pltpu.VMEM((ROWS, WIDTH), bf16),
            pltpu.VMEM((ROWS, WIDTH), bf16),
            pltpu.VMEM((ROWS, WIDTH), bf16),
            pltpu.VMEM((ROWS, WIDTH), bf16),
            pltpu.VMEM((ROWS, WIDTH), bf16),
            pltpu.VMEM((ROWS, WIDTH), bf16),
            pltpu.VMEM((ROWS, WIDTH), bf16),
            pltpu.VMEM((ROWS, WIDTH), bf16),
            pltpu.VMEM((ROWS, WIDTH), f32),
            dma((4,)), dma((CHUNKS,)),
            dma((CHUNKS, 3)), dma((CHUNKS, 3)),
            dma((3,)), dma((3,)),
            dma((PARTS, 3)), dma((PARTS, 3)),
            dma((1,)), dma((1,)),
            dma((CHUNKS,)), dma((CHUNKS,)),
            dma((blocks,)), dma((blocks,)),
            dma((blocks,)), dma((blocks,)),
            dma((blocks,)), dma((blocks,)),
            dma((2, blocks)),
        ],
        compiler_params=pltpu.CompilerParams(
            collective_id=power, has_side_effects=True, vmem_limit_bytes=48 * 2**20
        ),
        name=f"step_hop{hop}",
    )(hidden, cotangent, ids, params, momentum)


PLANS = (
    ("even", (4, 4), 2),
    ("mixed", (4, 10), 10),
    ("relay", (10, 10), 10),
    ("direct", (0, 0), 0),
)


def on_device(hidden_in, cotangent, token_ids, params, momentum, step_index):
    branches = [partial(step_call, power) for power in range(4)]
    new_params, new_momentum = lax.switch(
        step_index % 4, branches, hidden_in[0], cotangent[0], token_ids, params[0], momentum[0]
    )
    return (new_params[None], new_momentum[None])


def solution(mesh):
    in_specs = (
        P("rep", "shard", None),
        P("rep", "shard", None),
        P("rep", "shard"),
        P("rep", "shard", None),
        P("rep", "shard", None),
        P(),
    )
    out_specs = (P("rep", "shard", None), P("rep", "shard", None))
    return jax.shard_map(
        on_device, mesh=mesh, in_specs=in_specs, out_specs=out_specs, check_vma=False
    )
```

```python
from functools import partial

import jax
import jax.numpy as jnp
from jax import lax
from jax.experimental import pallas as pl
from jax.experimental.pallas import tpu as pltpu
from jax.sharding import PartitionSpec as P

MOMENTUM_DECAY = 0.9
STEP_SIZE = 0.1
MESH = pl.DeviceIdType.MESH

N_REP = 32
N_SHARD = 8
RING = 4
DEPTH = 8
TOK = 256
ROWS = 640
WIDTH = 1024
CHUNKS = 5
CHUNK = ROWS // CHUNKS
PARTS = 4
PART = WIDTH // PARTS
SHARE = 0.5 * MOMENTUM_DECAY
FEED = (
    ("mask", 0), ("tok", 0), ("tok", 1), ("mask", 1), ("tok", 2), ("mask", 2), ("tok", 3), ("mask", 3), ("tok", 4),
)


def block_order():
    order, chunks, parts = [], [], []
    for kind, index in FEED:
        if kind == "mask":
            order += [(c, index) for c in chunks]
            parts.append(index)
        else:
            order += [(index, q) for q in parts]
            chunks.append(index)
    return order


def step_kernel(
    hop, route, lags, late,
    hidden, cotangent, ids, params, momentum, out_params, out_momentum,
    tokens, turned, own_tokens, masked, cot, params32, params16, mom, peer_params, peer_mom,
    sums, middle, halfway, arrived, own,
    load_sem, load_tok_sem, tok_send, tok_recv, own_send, own_recv, mask_send, mask_recv,
    param_send, param_recv, mom_send, mom_recv, first_send, first_recv, second_send, second_recv,
    way_recv, way_send, store_sem,
):
    order = block_order()
    rep, shard = lax.axis_index("rep"), lax.axis_index("shard")
    half, place = shard // RING, shard % RING
    other_half = 1 - half
    low = (rep // 2) % 4
    across = other_half * RING + place
    ahead, behind = (rep + hop) % N_REP, (rep + N_REP - hop) % N_REP

    def along(distance):
        return (rep, half * RING + (place + distance) % RING)

    def along_z(distance):
        z = (half * 4 + low + distance + DEPTH) % DEPTH
        return ((rep // 8) * 8 + (z % 4) * 2 + rep % 2, (z // 4) * RING + place)

    def columns(which_half, distance, start, size):
        first = (which_half * RING + (place + distance) % RING) * ROWS + start
        return pl.ds(pl.multiple_of(first, 128), size)

    def local(src, dst, sem):
        copy = pltpu.make_async_copy(src, dst, sem)
        copy.start()
        return copy

    load_cot = local(cotangent, cot, load_sem.at[0])
    load_params = local(params, params32, load_sem.at[1])
    load_tok = [
        local(hidden.at[:, columns(other_half, 0, c * CHUNK, CHUNK)], tokens.at[c, 0], load_tok_sem.at[c])
        for c in range(CHUNKS)
    ]
    load_own = local(hidden.at[:, columns(half, 0, 0, ROWS)], own_tokens.at[0], load_sem.at[2])
    load_mom = local(momentum, mom, load_sem.at[3])

    def where(test, run):
        if isinstance(test, bool):
            if test:
                run()
        else:
            pl.when(test)(run)

    direct = route == "direct"
    always = route == "relay"

    def relayed(c, replica):
        if direct or always:
            return always
        if route == "even":
            return replica % 2 == 0
        return c % 2 == 0 or (replica // 2) % 4 == 0

    def otherwise(test):
        return not test if isinstance(test, bool) else jnp.logical_not(test)

    partners = [along(1), along(2), along(3), (ahead, shard), (behind, shard)]
    if direct:
        partners.append((rep, across))
    else:
        partners += [(behind, across), (ahead, across)]
        if not always:
            partners += [along_z(2), along_z(-2)]
    barrier = pltpu.get_barrier_semaphore()
    for partner in partners:
        pl.semaphore_signal(barrier, inc=1, device_id=partner, device_id_type=MESH)

    relay_first, relay_second = (behind, across), (ahead, shard)
    way_first = along_z(jnp.where(low >= 1, -2, 2))
    way_second = along_z(jnp.where(low == 2, 2, -2))
    way_rep = way_second[0]

    load_cot.wait()
    row = lax.broadcasted_iota(jnp.int32, (TOK, TOK), 0)
    col = lax.broadcasted_iota(jnp.int32, (TOK, TOK), 1)
    keep = jnp.logical_and(row == col, jnp.broadcast_to(ids[...], (TOK, TOK)) != 0)
    select = jnp.where(keep, 1.0, 0.0).astype(jnp.bfloat16)
    for q in range(PARTS):
        masked[q, 0] = jnp.dot(
            select, cot[:, q * PART:(q + 1) * PART], preferred_element_type=jnp.float32
        ).astype(jnp.bfloat16)

    load_params.wait()

    @pl.loop(0, CHUNKS)
    def _(c):
        rows = pl.ds(pl.multiple_of(c * CHUNK, CHUNK), CHUNK)
        params16[rows] = params32[rows].astype(jnp.bfloat16)

    pl.semaphore_wait(barrier, len(partners))

    def remote(src, dst, send, recv, device):
        return pltpu.make_async_remote_copy(
            src_ref=src, dst_ref=dst, send_sem=send, recv_sem=recv,
            device_id=device, device_id_type=MESH,
        )

    feed = {}

    def give(kind, index):
        feed[kind, index] = []
        for d in (1, 3, 2):
            if kind == "mask":
                copy = remote(
                    masked.at[index, 0], masked.at[index, d],
                    mask_send.at[index, d - 1], mask_recv.at[index, d - 1], along(d),
                )
            else:
                copy = remote(
                    hidden.at[:, columns(other_half, d, index * CHUNK, CHUNK)], tokens.at[index, d],
                    tok_send.at[index, d - 1], tok_recv.at[index, d - 1], along(d),
                )
            copy.start()
            feed[kind, index].append(copy)

    for item in FEED[:2]:
        give(*item)

    send_params = remote(params16, peer_params, param_send.at[0], param_recv.at[0], (ahead, shard))
    send_params.start()

    def send_mom(c):
        rows = pl.ds(c * CHUNK, CHUNK)
        return remote(momentum.at[rows], peer_mom.at[rows], mom_send.at[c], mom_recv.at[c], (ahead, shard))

    for c in range(CHUNKS):
        where(otherwise(relayed(c, ahead)), send_mom(c).start)

    for item in FEED[2:]:
        give(*item)

    send_own = [
        remote(
            hidden.at[:, columns(half, d, 0, ROWS)], own_tokens.at[d], own_send.at[d - 1], own_recv.at[d - 1], along(d)
        )
        for d in (1, 3, 2)
    ]
    for copy in send_own:
        copy.start()
    load_mom.wait()

    def block(c, q):
        return (pl.ds(c * CHUNK, CHUNK), pl.ds(q * PART, PART))

    def number(c, q):
        return c * PARTS + q

    def straight(c, q):
        i = number(c, q)
        return remote(sums.at[i], arrived.at[i], first_send.at[i], first_recv.at[i], (rep, across))

    def relay_leg(c, q):
        i = number(c, q)
        return remote(sums.at[i], middle.at[i], first_send.at[i], first_recv.at[i], relay_first)

    def way_leg(c, q):
        i = number(c, q)
        return remote(sums.at[i], halfway.at[i], first_send.at[i], way_recv.at[i], way_first)

    def relay_last(c, q):
        i = number(c, q)
        return remote(middle.at[i], arrived.at[i], second_send.at[i], second_recv.at[i], relay_second)

    def way_last(c, q):
        i = number(c, q)
        return remote(halfway.at[i], arrived.at[i], way_send.at[i], second_recv.at[i], way_second)

    def leave(c, q):
        if direct:
            straight(c, q).start()
        else:
            where(relayed(c, rep), relay_leg(c, q).start)
            where(otherwise(relayed(c, rep)), way_leg(c, q).start)

    have = set()

    def pass_relay(c, q):
        def run():
            at, i = block(c, q), number(c, q)
            relay_leg(c, q).wait_recv()
            middle[i] = (middle[i].astype(jnp.float32) + SHARE * mom[at].astype(jnp.float32)).astype(jnp.bfloat16)
            relay_last(c, q).start()

        where(relayed(c, ahead), run)

    def pass_way(c, q):
        def run():
            way_leg(c, q).wait_recv()
            way_last(c, q).start()

        where(otherwise(relayed(c, way_rep)), run)

    passed = [0, 0]

    def pass_until(*limits):
        if direct:
            return
        for i in range(len(order)):
            for k, run in enumerate((pass_way, pass_relay)):
                if passed[k] == i and i < limits[k]:
                    run(*order[i])
                    passed[k] = i + 1

    def need(kind, index):
        if (kind, index) in have:
            return
        have.add((kind, index))
        for copy in feed[kind, index]:
            copy.wait_recv()
        if kind == "tok":
            load_tok[index].wait()
            turned[index] = tokens[index].reshape(RING * TOK, CHUNK).T

    for i, (c, q) in enumerate(order):
        need("mask", q)
        need("tok", c)
        sums[number(c, q)] = jnp.dot(
            turned[c], masked[q].reshape(RING * TOK, PART), preferred_element_type=jnp.float32
        ).astype(jnp.bfloat16)
        leave(c, q)
        pass_until(i + 1 - lags[0], i + 1 - lags[1])

    pass_until(len(order) - late, len(order) - late)

    for copy in send_own:
        copy.wait_recv()
    load_own.wait()

    @pl.loop(0, CHUNKS)
    def _(c):
        rows = pl.ds(pl.multiple_of(c * CHUNK, CHUNK), CHUNK)
        left = own_tokens[:, :, rows].reshape(RING * TOK, CHUNK).T
        for q in range(PARTS):
            cols = pl.ds(q * PART, PART)
            own[rows, cols] = jnp.dot(
                left, masked[q].reshape(RING * TOK, PART), preferred_element_type=jnp.float32
            ) + SHARE * mom[rows, cols].astype(jnp.float32)

    pass_until(len(order), len(order))

    send_params.wait_recv()

    for c in range(CHUNKS):
        def add_peer(c=c):
            rows = pl.ds(c * CHUNK, CHUNK)
            send_mom(c).wait_recv()
            own[rows] = own[rows] + SHARE * peer_mom[rows].astype(jnp.float32)

        where(otherwise(relayed(c, rep)), add_peer)
    stores = []
    for c, q in order:
        at, i = block(c, q), number(c, q)
        if direct:
            straight(c, q).wait_recv()
        else:
            relay_last(c, q).wait_recv()
        moment = own[at] + arrived[i].astype(jnp.float32)
        mixed = 0.5 * (params32[at] + peer_params[at].astype(jnp.float32))
        params32[at] = mixed - STEP_SIZE * moment
        mom[at] = moment.astype(jnp.bfloat16)
        stores.append(local(params32.at[at], out_params.at[at], store_sem.at[0, i]))
        stores.append(local(mom.at[at], out_momentum.at[at], store_sem.at[1, i]))

    for copies in feed.values():
        for copy in copies:
            copy.wait_send()
    for copy in send_own + [send_params]:
        copy.wait_send()
    for c in range(CHUNKS):
        where(otherwise(relayed(c, ahead)), send_mom(c).wait_send)
    for c, q in order:
        straight(c, q).wait_send()
        if not direct:
            where(relayed(c, ahead), relay_last(c, q).wait_send)
            where(otherwise(relayed(c, way_rep)), way_last(c, q).wait_send)
    for copy in stores:
        copy.wait()


def step_call(power, hidden, cotangent, ids, params, momentum):
    hop = 2**power
    anywhere = pl.BlockSpec(memory_space=pl.ANY)
    bf16, f32, dma = jnp.bfloat16, jnp.float32, pltpu.SemaphoreType.DMA
    blocks = CHUNKS * PARTS
    return pl.pallas_call(
        partial(step_kernel, hop, *PLANS[power]),
        out_shape=(
            jax.ShapeDtypeStruct((ROWS, WIDTH), f32),
            jax.ShapeDtypeStruct((ROWS, WIDTH), bf16),
        ),
        in_specs=[anywhere, anywhere, pl.BlockSpec(memory_space=pltpu.VMEM), anywhere, anywhere],
        out_specs=(anywhere, anywhere),
        scratch_shapes=[
            pltpu.VMEM((CHUNKS, RING, TOK, CHUNK), bf16),
            pltpu.VMEM((CHUNKS, CHUNK, RING * TOK), bf16),
            pltpu.VMEM((RING, TOK, ROWS), bf16),
            pltpu.VMEM((PARTS, RING, TOK, PART), bf16),
            pltpu.VMEM((TOK, WIDTH), bf16),
            pltpu.VMEM((ROWS, WIDTH), f32),
            pltpu.VMEM((ROWS, WIDTH), bf16),
            pltpu.VMEM((ROWS, WIDTH), bf16),
            pltpu.VMEM((ROWS, WIDTH), bf16),
            pltpu.VMEM((ROWS, WIDTH), bf16),
            pltpu.VMEM((blocks, CHUNK, PART), bf16),
            pltpu.VMEM((blocks, CHUNK, PART), bf16),
            pltpu.VMEM((blocks, CHUNK, PART), bf16),
            pltpu.VMEM((blocks, CHUNK, PART), bf16),
            pltpu.VMEM((ROWS, WIDTH), f32),
            dma((4,)), dma((CHUNKS,)),
            dma((CHUNKS, 3)), dma((CHUNKS, 3)),
            dma((3,)), dma((3,)),
            dma((PARTS, 3)), dma((PARTS, 3)),
            dma((1,)), dma((1,)),
            dma((CHUNKS,)), dma((CHUNKS,)),
            dma((blocks,)), dma((blocks,)),
            dma((blocks,)), dma((blocks,)),
            dma((blocks,)), dma((blocks,)),
            dma((2, blocks)),
        ],
        compiler_params=pltpu.CompilerParams(
            collective_id=power, has_side_effects=True, vmem_limit_bytes=48 * 2**20
        ),
        name=f"step_hop{hop}",
    )(hidden, cotangent, ids, params, momentum)


PLANS = (
    ("even", (4, 4), 2),
    ("mixed", (4, 10), 10),
    ("relay", (10, 10), 10),
    ("direct", (0, 0), 0),
)


def on_device(hidden_in, cotangent, token_ids, params, momentum, step_index):
    branches = [partial(step_call, power) for power in range(4)]
    new_params, new_momentum = lax.switch(
        step_index % 4, branches, hidden_in[0], cotangent[0], token_ids, params[0], momentum[0]
    )
    return (new_params[None], new_momentum[None])


def solution(mesh):
    in_specs = (
        P("rep", "shard", None),
        P("rep", "shard", None),
        P("rep", "shard"),
        P("rep", "shard", None),
        P("rep", "shard", None),
        P(),
    )
    out_specs = (P("rep", "shard", None), P("rep", "shard", None))
    return jax.shard_map(
        on_device, mesh=mesh, in_specs=in_specs, out_specs=out_specs, check_vma=False
    )
```
